32 devices in a mesh: parts: 2 (over x), dp: 16 (over z, y, core).
Axes of the slice: x: 2, y: 2, z: 4, core: 2. Of those that a mesh axis runs over, the one named last changes fastest.
Arguments:
- grads: bfloat16 [2048, 3, 10240], P(('parts', 'dp')), parts along dimension 0, may hold values from -4 to 4
- valid: bfloat16 [32, 3, 10240], P(('parts', 'dp')), parts along dimension 0, may hold values from -6 to 6
Outputs:
- weighted: float32 [32, 3, 10240], P(('parts', 'dp')), parts along dimension 0
The draws below stay inside these ranges and needn't reach their ends.
There are 2 independent parts, one for each index of `parts`. The reference program is written for one: setup_inputs(seed, part) draws one part's arguments, and reference() takes and returns one part's arrays. A program takes and returns all parts, laid end to end along the dimension named above; each array names one. Nothing has to cross between parts.
All inputs are finite; a program needn't handle non-finite values.
Results may differ from the reference program's by a relative error of at most 0.0026.
Values may be sent and summed in bfloat16 or wider, within the bound.
A program may use at most 64 MiB of HBM per device.

```python
import jax
import jax.numpy as jnp

W = 10240
LAYERS = 3
EXAMPLES = 1024
NV = 16


def draw_grads(key, part):
    key = jax.random.fold_in(key, 7)
    keys = jax.random.split(key, 3)
    shape = (EXAMPLES, LAYERS, W)
    rows = jnp.exp(jax.random.uniform(keys[0], (EXAMPLES, LAYERS, 1), jnp.float32) * jnp.log(10.0))
    index = jnp.arange(EXAMPLES, dtype=jnp.float32)[:, None, None]
    rise = jnp.sqrt(1.0 + 2.0 * index / max(EXAMPLES - 1, 1))
    cols = jnp.exp(jax.random.uniform(keys[1], (1, LAYERS, W), jnp.float32) * jnp.log(10.0))
    base = jnp.clip(jax.random.normal(keys[2], shape, jnp.float32), -5.0, 5.0)
    values = 0.003 * base * rows * rise * cols
    return jnp.clip(values, -4.0, 4.0).astype(jnp.bfloat16)


def block_levels(key, dims, shards, smallest, largest):
    def one(dim, shards_of):
        heights = jax.random.uniform(jax.random.fold_in(jax.random.fold_in(key, 6), dim), (shards_of,), jnp.float32, smallest / len(shards), largest / len(shards))
        return jnp.repeat(jnp.exp(heights), dims[dim] // shards_of).reshape((-1,) + (1,) * (len(dims) - dim - 1))

    level = one(*shards[0])
    for cut in shards[1:]:
        level = level * one(*cut)
    return level


def normal_values(rng, extent, deviation, reach, cuts=(), kind=jnp.bfloat16):
    result = jax.random.normal(rng, extent, jnp.float32) * deviation
    if len(cuts) > 0:
        result = block_levels(rng, extent, cuts, -0.22, 0.18) * result
    return jnp.clip(result, min=-reach, max=reach).astype(kind)


def setup_inputs(seed: int = 0, part: int = 0) -> dict:
    key_of = jax.random.split(jax.random.key(seed), 3)
    part_splits = jax.random.split(jax.random.fold_in(key_of[2], part), 3)
    return {
        "grads": draw_grads(jax.random.fold_in(jax.random.fold_in(key_of[2], part), 71), part),
        "valid": normal_values(part_splits[1], (NV, LAYERS, W), 1.0, 6.0, ((0, 16),)),
    }


def reference(grads, valid):
    outs = []
    for layer in range(LAYERS):
        g_layer = grads[:, layer, :]
        v_layer = valid[:, layer, :]
        norms = jnp.sum(g_layer.astype(jnp.float32) * g_layer.astype(jnp.float32), axis=1)
        damping = 0.1 * jnp.sum(norms) / EXAMPLES
        dots = jnp.dot(g_layer, v_layer.T, preferred_element_type=jnp.float32)
        coef = (dots / (damping + norms[:, None])).astype(jnp.bfloat16)
        outs.append(jnp.dot(coef.T, g_layer, preferred_element_type=jnp.float32))
    return jnp.stack(outs, axis=1)
```

```python
import functools

import jax
import jax.numpy as jnp
from jax import lax
from jax.experimental import pallas as pl
from jax.experimental.pallas import tpu as pltpu
from jax.sharding import PartitionSpec as P

MESH = pl.DeviceIdType.MESH
LANES = 128


def coefficients(grads, block, damping, norms):
    dots = jnp.einsum("elw,vlw->lev", grads, block, preferred_element_type=jnp.float32)
    return (dots / (damping[:, None, None] + norms.T[:, :, None])).astype(jnp.bfloat16)


def shards(grads, valid):
    local_rows = grads.shape[0]
    norms = jnp.einsum("elw,elw->el", grads, grads, preferred_element_type=jnp.float32)
    total = lax.psum(jnp.sum(norms, axis=0), "dp")
    damping = 0.1 * total / (local_rows * lax.axis_size("dp"))
    everything = lax.all_gather(valid, "dp", axis=0, tiled=True)
    coef = coefficients(grads, everything, damping, norms)
    return lax.psum_scatter(
        jnp.einsum("lev,elw->vlw", coef, grads, preferred_element_type=jnp.float32),
        "dp",
        scatter_dimension=0,
        tiled=True,
    )


NC, NY, NZ = 2, 2, 4
N = NC * NY * NZ
HALF = NY * NZ


def slot(dc, dy, dz):
    return (dc * NY + dy) * NZ + dz % NZ


def kernel(
    grads_hbm, valid_ref, out_ref,
    grads, row_form, everything, v_form, norms, total, totals, partial, from_core, to_y, from_y, to_z, from_z, mine,
    load_sem, gather_send, gather_recv, total_send, total_recv,
    core_send, core_recv, y_send, y_recv, z_send, z_recv,
):
    layers, examples, width = grads_hbm.shape
    chunks = width // LANES
    part, me = lax.axis_index("parts"), lax.axis_index("dp")
    c, y, z = me % NC, (me // NC) % NY, me // (NC * NY)

    def device(dc, dy, dz):
        pc = 1 - c if dc else c
        py = 1 - y if dy else y
        pz = (z + dz) % NZ
        return (part, (pz * NY + py) * NC + pc)

    def copy(src, dst, send, recv, to):
        return pltpu.make_async_remote_copy(
            src_ref=src, dst_ref=dst, send_sem=send, recv_sem=recv, device_id=to, device_id_type=MESH
        )

    sent = []

    def start(*args):
        one = copy(*args)
        one.start()
        sent.append(one)

    offsets = [(dc, dy, dz) for dc in range(NC) for dy in range(NY) for dz in range(NZ) if (dc, dy, dz) != (0, 0, 0)]

    loads = [pltpu.make_async_copy(grads_hbm.at[l], grads.at[l], load_sem.at[l]) for l in range(layers)]
    for load in loads:
        load.start()

    barrier = pltpu.get_barrier_semaphore()
    for offset in offsets:
        pl.semaphore_signal(barrier, inc=1, device_id=device(*offset), device_id_type=MESH)

    for j in range(chunks):
        row_form[8 * j : 8 * j + layers, :] = valid_ref[:, LANES * j : LANES * (j + 1)].astype(jnp.float32)
    for l in range(layers):
        everything[l, 0] = row_form[pl.ds(l, chunks, stride=8), :].astype(jnp.bfloat16)
    pl.semaphore_wait(barrier, N - 1)

    counter = [0] * layers

    def give(l, src, dst, to):
        start(everything.at[l, src], everything.at[l, dst], gather_send.at[l, counter[l]], gather_recv.at[l, dst], to)
        counter[l] += 1

    arrived = set()

    def take(l, k):
        if (l, k) not in arrived:
            arrived.add((l, k))
            copy(
                everything.at[l, k], everything.at[l, k], gather_send.at[l, 0], gather_recv.at[l, k], device(1, 0, 0)
            ).wait_recv()

    def gather_1(l):
        for dz in (2, 1, 3):
            give(l, 0, slot(0, 0, -dz), device(0, 0, dz))
        give(l, 0, slot(0, 1, 0), device(0, 1, 0))
        give(l, 0, slot(1, 0, 0), device(1, 0, 0))

    def gather_2(l):
        for dz in (1, 3, 2):
            k = slot(0, 0, dz)
            take(l, k)
            give(l, k, slot(0, 1, dz), device(0, 1, 0))
            give(l, k, slot(1, 0, dz), device(1, 0, 0))

    def gather_3(l):
        for dz in (0, 1, 3, 2):
            k = slot(0, 1, dz)
            take(l, k)
            give(l, k, slot(1, 1, dz), device(1, 0, 0))

    def norm(l):
        loads[l].wait()
        wide = 8 * LANES if width % (8 * LANES) == 0 else LANES

        def body(i, acc):
            x = grads[l, :, pl.ds(pl.multiple_of(i * wide, wide), wide)].astype(jnp.float32)
            x = x * x
            for j in range(wide // LANES):
                acc = acc + x[:, LANES * j : LANES * (j + 1)]
            return acc

        acc = lax.fori_loop(0, width // wide, body, jnp.zeros((examples, LANES), jnp.float32))
        each = jnp.sum(acc, axis=1, keepdims=True)
        norms[l] = jnp.broadcast_to(each, (examples, LANES))
        total[l : l + 1, :] = jnp.broadcast_to(jnp.sum(each, axis=0, keepdims=True), (1, LANES))

    def send_totals():
        for dc, dy, dz in offsets:
            k = slot(dc, dy, -dz)
            start(total, totals.at[k], total_send.at[k], total_recv.at[k], device(dc, dy, dz))

    def take_totals():
        for dc, dy, dz in offsets:
            k = slot(dc, dy, dz)
            copy(total, totals.at[k], total_send.at[k], total_recv.at[k], device(1, 0, 0)).wait_recv()
        acc = total[...]
        for dc, dy, dz in offsets:
            acc = acc + totals[slot(dc, dy, dz)]
        total_damping = 0.1 * acc / (examples * N)
        return total_damping

    def form(l):
        for k in range(N):
            if k:
                take(l, k)
            v_form[pl.ds(k, chunks, stride=N), :] = everything[l, k].astype(jnp.float32)

    def dots(l):
        wide = 2560 if width % 2560 == 0 else width
        acc = jnp.zeros((examples, N), jnp.float32)
        for i in range(width // wide):
            block = jnp.concatenate(
                [v_form[N * j : N * (j + 1), :] for j in range(i * wide // LANES, (i + 1) * wide // LANES)], axis=1
            ).astype(jnp.bfloat16)
            acc = acc + lax.dot_general(
                grads[l, :, i * wide : (i + 1) * wide], block, (((1,), (1,)), ((), ())),
                preferred_element_type=jnp.float32,
            )
        return acc

    def weigh(l, product, damping):
        coef = product / (damping[l : l + 1, :N] + norms[l, :, :N])
        coef = coef.T.astype(jnp.bfloat16)
        wide = 1280 if width % 1280 == 0 else width
        for i in range(width // wide):
            result = jnp.dot(coef, grads[l, :, i * wide : (i + 1) * wide], preferred_element_type=jnp.float32)
            for j in range(wide // LANES):
                at = i * wide // LANES + j
                for dc in range(NC):
                    partial[l, dc, HALF * at : HALF * (at + 1), :] = result[HALF * dc : HALF * (dc + 1), LANES * j : LANES * (j + 1)]
        start(partial.at[l, 1], from_core.at[l], core_send.at[l], core_recv.at[l], device(1, 0, 0))

    def scatter_y(l):
        copy(partial.at[l, 1], from_core.at[l], core_send.at[l], core_recv.at[l], device(1, 0, 0)).wait_recv()
        for dz in range(NZ):
            rows = pl.ds(slot(0, 1, dz), chunks, stride=HALF)
            to_y[l, dz] = (partial[l, 0, rows, :] + from_core[l, rows, :]).astype(jnp.bfloat16)
        start(to_y.at[l], from_y.at[l], y_send.at[l], y_recv.at[l], device(0, 1, 0))

    def scatter_z(l):
        copy(to_y.at[l], from_y.at[l], y_send.at[l], y_recv.at[l], device(0, 1, 0)).wait_recv()
        for dz in (2, 1, 3, 0):
            rows = pl.ds(slot(0, 0, dz), chunks, stride=HALF)
            part_sum = partial[l, 0, rows, :] + from_core[l, rows, :] + from_y[l, dz].astype(jnp.float32)
            if dz:
                to_z[l, dz - 1] = part_sum.astype(jnp.bfloat16)
                at = NZ - dz - 1
                start(to_z.at[l, dz - 1], from_z.at[l, at], z_send.at[l, dz - 1], z_recv.at[l, at], device(0, 0, dz))
            else:
                mine[l] = part_sum

    def finish(l):
        acc = mine[l]
        for i in range(NZ - 1):
            copy(to_z.at[l, i], from_z.at[l, i], z_send.at[l, i], z_recv.at[l, i], device(0, 1, 0)).wait_recv()
            acc = acc + from_z[l, i].astype(jnp.float32)
        out_ref[l] = acc

    total[...] = jnp.zeros_like(total)
    for l in range(layers):
        gather_1(l)
    for l in range(layers):
        norm(l)
        gather_2(l)
        if l:
            gather_3(l - 1)
    send_totals()
    damping = None
    for l in range(layers):
        form(l)
        product = dots(l)
        if l == 0:
            damping = take_totals()
        weigh(l, product, damping)
        if l == 0:
            gather_3(layers - 1)
        if l >= 1:
            scatter_y(l - 1)
        if l >= 2:
            scatter_z(l - 2)
    scatter_y(layers - 1)
    for l in range(max(layers - 2, 0), layers):
        scatter_z(l)
    for l in range(layers):
        finish(l)
    for one in sent:
        one.wait_send()


def fused(grads, valid):
    examples, layers, width = grads.shape
    chunks = width // LANES
    bf16, f32 = jnp.bfloat16, jnp.float32
    dma = pltpu.SemaphoreType.DMA
    out = pl.pallas_call(
        kernel,
        out_shape=jax.ShapeDtypeStruct((layers, chunks, LANES), f32),
        in_specs=[pl.BlockSpec(memory_space=pl.ANY), pl.BlockSpec(memory_space=pltpu.VMEM)],
        out_specs=pl.BlockSpec(memory_space=pltpu.VMEM),
        scratch_shapes=[
            pltpu.VMEM((layers, examples, width), bf16),
            pltpu.VMEM((chunks * 8, LANES), f32),
            pltpu.VMEM((layers, N, chunks, LANES), bf16),
            pltpu.VMEM((chunks * N, LANES), f32),
            pltpu.VMEM((layers, examples, LANES), f32),
            pltpu.VMEM((8, LANES), f32),
            pltpu.VMEM((N, 8, LANES), f32),
            pltpu.VMEM((layers, NC, chunks * HALF, LANES), f32),
            pltpu.VMEM((layers, chunks * HALF, LANES), f32),
            pltpu.VMEM((layers, NZ, chunks, LANES), bf16),
            pltpu.VMEM((layers, NZ, chunks, LANES), bf16),
            pltpu.VMEM((layers, NZ - 1, chunks, LANES), bf16),
            pltpu.VMEM((layers, NZ - 1, chunks, LANES), bf16),
            pltpu.VMEM((layers, chunks, LANES), f32),
            dma((layers,)),
            dma((layers, N)),
            dma((layers, N)),
            dma((N,)),
            dma((N,)),
            dma((layers,)),
            dma((layers,)),
            dma((layers,)),
            dma((layers,)),
            dma((layers, NZ - 1)),
            dma((layers, NZ - 1)),
        ],
        compiler_params=pltpu.CompilerParams(
            collective_id=0, has_side_effects=True, vmem_limit_bytes=48 * 1024 * 1024
        ),
    )(jnp.transpose(grads, (1, 0, 2)), valid.reshape(layers, width))
    return out.reshape(1, layers, width)


def solution(mesh):
    def step(grads, valid):
        fits = mesh.shape["dp"] == N and valid.shape[0] == 1 and grads.shape[2] % (16 * LANES) == 0
        return (fused if fits else shards)(grads, valid)

    return jax.shard_map(
        step,
        mesh=mesh,
        in_specs=(P(("parts", "dp"), None, None), P(("parts", "dp"), None, None)),
        out_specs=P(("parts", "dp"), None, None),
        check_vma=False,
    )
```

```python
import functools

import jax
import jax.numpy as jnp
from jax import lax
from jax.experimental import pallas as pl
from jax.experimental.pallas import tpu as pltpu
from jax.sharding import PartitionSpec as P

MESH = pl.DeviceIdType.MESH
LANES = 128


def coefficients(grads, block, damping, norms):
    dots = jnp.einsum("elw,vlw->lev", grads, block, preferred_element_type=jnp.float32)
    return (dots / (damping[:, None, None] + norms.T[:, :, None])).astype(jnp.bfloat16)


def shards(grads, valid):
    local_rows = grads.shape[0]
    norms = jnp.einsum("elw,elw->el", grads, grads, preferred_element_type=jnp.float32)
    total = lax.psum(jnp.sum(norms, axis=0), "dp")
    damping = 0.1 * total / (local_rows * lax.axis_size("dp"))
    everything = lax.all_gather(valid, "dp", axis=0, tiled=True)
    coef = coefficients(grads, everything, damping, norms)
    return lax.psum_scatter(
        jnp.einsum("lev,elw->vlw", coef, grads, preferred_element_type=jnp.float32),
        "dp",
        scatter_dimension=0,
        tiled=True,
    )


NC, NY, NZ = 2, 2, 4
N = NC * NY * NZ
HALF = NY * NZ


def slot(dc, dy, dz):
    return (dc * NY + dy) * NZ + dz % NZ


def kernel(
    grads_hbm, valid_hbm, out_ref,
    grads, valid_ref, row_form, everything, v_form, norms, total, totals, partial, from_core, to_y, from_y, to_z, from_z, mine,
    load_sem, valid_sem, gather_send, gather_recv, total_send, total_recv,
    core_send, core_recv, y_send, y_recv, z_send, z_recv,
):
    layers, examples, width = grads_hbm.shape
    chunks = width // LANES
    part, me = lax.axis_index("parts"), lax.axis_index("dp")
    c, y, z = me % NC, (me // NC) % NY, me // (NC * NY)

    def device(dc, dy, dz):
        pc = 1 - c if dc else c
        py = 1 - y if dy else y
        pz = (z + dz) % NZ
        return (part, (pz * NY + py) * NC + pc)

    def copy(src, dst, send, recv, to):
        return pltpu.make_async_remote_copy(
            src_ref=src, dst_ref=dst, send_sem=send, recv_sem=recv, device_id=to, device_id_type=MESH
        )

    sent = []

    def start(*args):
        one = copy(*args)
        one.start()
        sent.append(one)

    offsets = [(dc, dy, dz) for dc in range(NC) for dy in range(NY) for dz in range(NZ) if (dc, dy, dz) != (0, 0, 0)]

    barrier = pltpu.get_barrier_semaphore()
    for offset in offsets:
        pl.semaphore_signal(barrier, inc=1, device_id=device(*offset), device_id_type=MESH)

    load_valid = pltpu.make_async_copy(valid_hbm, valid_ref, valid_sem)
    load_valid.start()
    loads = [pltpu.make_async_copy(grads_hbm.at[l], grads.at[l], load_sem.at[l]) for l in range(layers)]
    for load in loads:
        load.start()

    load_valid.wait()
    for j in range(chunks):
        row_form[8 * j : 8 * j + layers, :] = valid_ref[:, LANES * j : LANES * (j + 1)].astype(jnp.float32)
    for l in range(layers):
        everything[l, 0] = row_form[pl.ds(l, chunks, stride=8), :].astype(jnp.bfloat16)

    counter = [0] * layers

    def give(l, src, dst, to):
        start(everything.at[l, src], everything.at[l, dst], gather_send.at[l, counter[l]], gather_recv.at[l, dst], to)
        counter[l] += 1

    arrived = set()

    def take(l, k):
        if (l, k) not in arrived:
            arrived.add((l, k))
            copy(
                everything.at[l, k], everything.at[l, k], gather_send.at[l, 0], gather_recv.at[l, k], device(1, 0, 0)
            ).wait_recv()

    def gather_1(l):
        for dz in (2, 1, 3):
            give(l, 0, slot(0, 0, -dz), device(0, 0, dz))
        give(l, 0, slot(0, 1, 0), device(0, 1, 0))
        give(l, 0, slot(1, 0, 0), device(1, 0, 0))

    def gather_2(l):
        for dz in (1, 3, 2):
            k = slot(0, 0, dz)
            take(l, k)
            give(l, k, slot(0, 1, dz), device(0, 1, 0))
            give(l, k, slot(1, 0, dz), device(1, 0, 0))

    def gather_3(l):
        for dz in (0, 1, 3, 2):
            k = slot(0, 1, dz)
            take(l, k)
            give(l, k, slot(1, 1, dz), device(1, 0, 0))

    def norm(l):
        loads[l].wait()
        wide = 8 * LANES if width % (8 * LANES) == 0 else LANES

        def body(i, acc):
            x = grads[l, :, pl.ds(pl.multiple_of(i * wide, wide), wide)].astype(jnp.float32)
            x = x * x
            for j in range(wide // LANES):
                acc = acc + x[:, LANES * j : LANES * (j + 1)]
            return acc

        acc = lax.fori_loop(0, width // wide, body, jnp.zeros((examples, LANES), jnp.float32))
        each = jnp.sum(acc, axis=1, keepdims=True)
        norms[l] = jnp.broadcast_to(each, (examples, LANES))
        return jnp.broadcast_to(jnp.sum(each, axis=0, keepdims=True), (1, LANES))

    def send_totals():
        for dc, dy, dz in offsets:
            k = slot(dc, dy, -dz)
            start(total, totals.at[k], total_send.at[k], total_recv.at[k], device(dc, dy, dz))

    def take_totals():
        for dc, dy, dz in offsets:
            k = slot(dc, dy, dz)
            copy(total, totals.at[k], total_send.at[k], total_recv.at[k], device(1, 0, 0)).wait_recv()
        acc = total[...]
        for dc, dy, dz in offsets:
            acc = acc + totals[slot(dc, dy, dz)]
        total_damping = 0.1 * acc / (examples * N)
        return total_damping

    def form(l):
        for k in range(N):
            if k:
                take(l, k)
            v_form[pl.ds(k, chunks, stride=N), :] = everything[l, k].astype(jnp.float32)

    def dots(l):
        wide = 2560 if width % 2560 == 0 else width
        acc = jnp.zeros((examples, N), jnp.float32)
        for i in range(width // wide):
            block = jnp.concatenate(
                [v_form[N * j : N * (j + 1), :] for j in range(i * wide // LANES, (i + 1) * wide // LANES)], axis=1
            ).astype(jnp.bfloat16)
            acc = acc + lax.dot_general(
                grads[l, :, i * wide : (i + 1) * wide], block, (((1,), (1,)), ((), ())),
                preferred_element_type=jnp.float32,
            )
        return acc

    def weigh(l, product, damping):
        coef = product / (damping[:, l : l + 1] + norms[l, :, :N])
        coef = coef.T.astype(jnp.bfloat16)
        wide = 1280 if width % 1280 == 0 else width
        for i in range(width // wide):
            result = jnp.dot(coef, grads[l, :, i * wide : (i + 1) * wide], preferred_element_type=jnp.float32)
            for j in range(wide // LANES):
                at = i * wide // LANES + j
                for dc in range(NC):
                    partial[l, dc, HALF * at : HALF * (at + 1), :] = result[HALF * dc : HALF * (dc + 1), LANES * j : LANES * (j + 1)]
        start(partial.at[l, 1], from_core.at[l], core_send.at[l], core_recv.at[l], device(1, 0, 0))

    def scatter_y(l):
        copy(partial.at[l, 1], from_core.at[l], core_send.at[l], core_recv.at[l], device(1, 0, 0)).wait_recv()
        for dz in range(NZ):
            rows = pl.ds(slot(0, 1, dz), chunks, stride=HALF)
            to_y[l, dz] = (partial[l, 0, rows, :] + from_core[l, rows, :]).astype(jnp.bfloat16)
        start(to_y.at[l], from_y.at[l], y_send.at[l], y_recv.at[l], device(0, 1, 0))

    def scatter_z(l):
        copy(to_y.at[l], from_y.at[l], y_send.at[l], y_recv.at[l], device(0, 1, 0)).wait_recv()
        for dz in (2, 1, 3, 0):
            rows = pl.ds(slot(0, 0, dz), chunks, stride=HALF)
            part_sum = partial[l, 0, rows, :] + from_core[l, rows, :] + from_y[l, dz].astype(jnp.float32)
            if dz:
                to_z[l, dz - 1] = part_sum.astype(jnp.bfloat16)
                at = NZ - dz - 1
                start(to_z.at[l, dz - 1], from_z.at[l, at], z_send.at[l, dz - 1], z_recv.at[l, at], device(0, 0, dz))
            else:
                mine[l] = part_sum

    def finish(l):
        acc = mine[l]
        for i in range(NZ - 1):
            copy(to_z.at[l, i], from_z.at[l, i], z_send.at[l, i], z_recv.at[l, i], device(0, 1, 0)).wait_recv()
            acc = acc + from_z[l, i].astype(jnp.float32)
        out_ref[l] = acc

    lane = lax.broadcasted_iota(jnp.int32, (1, LANES), 1)
    row = jnp.zeros((1, LANES), jnp.float32)
    for l in range(layers):
        row = jnp.where(lane == l, norm(l), row)
    total[...] = row
    pl.semaphore_wait(barrier, N - 1)
    gather_1(0)
    send_totals()
    for l in range(1, layers):
        gather_1(l)
    for l in range(layers):
        gather_2(l)
        if l:
            gather_3(l - 1)
    damping = None
    for l in range(layers):
        form(l)
        product = dots(l)
        if l == 0:
            damping = take_totals()
        weigh(l, product, damping)
        if l == 0:
            gather_3(layers - 1)
        if l >= 1:
            scatter_y(l - 1)
        if l >= 2:
            scatter_z(l - 2)
    scatter_y(layers - 1)
    for l in range(max(layers - 2, 0), layers):
        scatter_z(l)
    for l in range(layers):
        finish(l)
    for one in sent:
        one.wait_send()


def fused(grads, valid):
    examples, layers, width = grads.shape
    chunks = width // LANES
    bf16, f32 = jnp.bfloat16, jnp.float32
    dma = pltpu.SemaphoreType.DMA
    out = pl.pallas_call(
        kernel,
        out_shape=jax.ShapeDtypeStruct((layers, chunks, LANES), f32),
        in_specs=[pl.BlockSpec(memory_space=pl.ANY), pl.BlockSpec(memory_space=pl.ANY)],
        out_specs=pl.BlockSpec(memory_space=pltpu.VMEM),
        scratch_shapes=[
            pltpu.VMEM((layers, examples, width), bf16),
            pltpu.VMEM((layers, width), bf16),
            pltpu.VMEM((chunks * 8, LANES), f32),
            pltpu.VMEM((layers, N, chunks, LANES), bf16),
            pltpu.VMEM((chunks * N, LANES), f32),
            pltpu.VMEM((layers, examples, LANES), f32),
            pltpu.VMEM((1, LANES), f32),
            pltpu.VMEM((N, 1, LANES), f32),
            pltpu.VMEM((layers, NC, chunks * HALF, LANES), f32),
            pltpu.VMEM((layers, chunks * HALF, LANES), f32),
            pltpu.VMEM((layers, NZ, chunks, LANES), bf16),
            pltpu.VMEM((layers, NZ, chunks, LANES), bf16),
            pltpu.VMEM((layers, NZ - 1, chunks, LANES), bf16),
            pltpu.VMEM((layers, NZ - 1, chunks, LANES), bf16),
            pltpu.VMEM((layers, chunks, LANES), f32),
            dma((layers,)),
            dma,
            dma((layers, N)),
            dma((layers, N)),
            dma((N,)),
            dma((N,)),
            dma((layers,)),
            dma((layers,)),
            dma((layers,)),
            dma((layers,)),
            dma((layers, NZ - 1)),
            dma((layers, NZ - 1)),
        ],
        compiler_params=pltpu.CompilerParams(
            collective_id=0, has_side_effects=True, vmem_limit_bytes=60 * 1024 * 1024
        ),
    )(jnp.transpose(grads, (1, 0, 2)), valid.reshape(layers, width))
    return out.reshape(1, layers, width)


def solution(mesh):
    def step(grads, valid):
        fits = mesh.shape["dp"] == N and valid.shape[0] == 1 and grads.shape[2] % (16 * LANES) == 0
        return (fused if fits else shards)(grads, valid)

    return jax.shard_map(
        step,
        mesh=mesh,
        in_specs=(P(("parts", "dp"), None, None), P(("parts", "dp"), None, None)),
        out_specs=P(("parts", "dp"), None, None),
        check_vma=False,
    )
```

```python
import functools

import jax
import jax.numpy as jnp
from jax import lax
from jax.experimental import pallas as pl
from jax.experimental.pallas import tpu as pltpu
from jax.sharding import PartitionSpec as P

MESH = pl.DeviceIdType.MESH
LANES = 128


def coefficients(grads, block, damping, norms):
    dots = jnp.einsum("elw,vlw->lev", grads, block, preferred_element_type=jnp.float32)
    return (dots / (damping[:, None, None] + norms.T[:, :, None])).astype(jnp.bfloat16)


def shards(grads, valid):
    local_rows = grads.shape[0]
    norms = jnp.einsum("elw,elw->el", grads, grads, preferred_element_type=jnp.float32)
    total = lax.psum(jnp.sum(norms, axis=0), "dp")
    damping = 0.1 * total / (local_rows * lax.axis_size("dp"))
    everything = lax.all_gather(valid, "dp", axis=0, tiled=True)
    coef = coefficients(grads, everything, damping, norms)
    return lax.psum_scatter(
        jnp.einsum("lev,elw->vlw", coef, grads, preferred_element_type=jnp.float32),
        "dp",
        scatter_dimension=0,
        tiled=True,
    )


NC, NY, NZ = 2, 2, 4
N = NC * NY * NZ
HALF = NY * NZ


def slot(dc, dy, dz):
    return (dc * NY + dy) * NZ + dz % NZ


def kernel(
    grads_hbm, valid_hbm, out_ref,
    grads, valid_ref, row_form, everything, v_form, norms, total, totals, partial, from_core, to_y, from_y, to_z, from_z, mine,
    load_sem, valid_sem, gather_send, gather_recv, total_send, total_recv,
    core_send, core_recv, y_send, y_recv, z_send, z_recv,
):
    layers, examples, width = grads_hbm.shape
    chunks = width // LANES
    part, me = lax.axis_index("parts"), lax.axis_index("dp")
    c, y, z = me % NC, (me // NC) % NY, me // (NC * NY)

    def device(dc, dy, dz):
        pc = 1 - c if dc else c
        py = 1 - y if dy else y
        pz = (z + dz) % NZ
        return (part, (pz * NY + py) * NC + pc)

    def copy(src, dst, send, recv, to):
        return pltpu.make_async_remote_copy(
            src_ref=src, dst_ref=dst, send_sem=send, recv_sem=recv, device_id=to, device_id_type=MESH
        )

    sent = []

    def start(*args):
        one = copy(*args)
        one.start()
        sent.append(one)

    offsets = [(0, 0, dz) for dz in (2, 1, 3)] + [(0, 1, 0), (1, 0, 0)]

    barrier = pltpu.get_barrier_semaphore()
    for offset in offsets:
        pl.semaphore_signal(barrier, inc=1, device_id=device(*offset), device_id_type=MESH)

    load_valid = pltpu.make_async_copy(valid_hbm, valid_ref, valid_sem)
    load_valid.start()
    loads = [pltpu.make_async_copy(grads_hbm.at[l], grads.at[l], load_sem.at[l]) for l in range(layers)]
    for load in loads:
        load.start()

    load_valid.wait()
    for j in range(chunks):
        row_form[8 * j : 8 * j + layers, :] = valid_ref[:, LANES * j : LANES * (j + 1)].astype(jnp.float32)
    for l in range(layers):
        everything[l, 0] = row_form[pl.ds(l, chunks, stride=8), :].astype(jnp.bfloat16)

    counter = [0] * layers

    def give(l, src, dst, to):
        start(everything.at[l, src], everything.at[l, dst], gather_send.at[l, counter[l]], gather_recv.at[l, dst], to)
        counter[l] += 1

    arrived = set()

    def take(l, k):
        if (l, k) not in arrived:
            arrived.add((l, k))
            copy(
                everything.at[l, k], everything.at[l, k], gather_send.at[l, 0], gather_recv.at[l, k], device(1, 0, 0)
            ).wait_recv()

    def gather_1(l):
        for dz in (1, 3, 2):
            give(l, 0, slot(0, 0, -dz), device(0, 0, dz))
        give(l, 0, slot(0, 1, 0), device(0, 1, 0))
        give(l, 0, slot(1, 0, 0), device(1, 0, 0))

    def gather_2(l):
        for dz in (1, 3, 2):
            k = slot(0, 0, dz)
            take(l, k)
            give(l, k, slot(0, 1, dz), device(0, 1, 0))
            give(l, k, slot(1, 0, dz), device(1, 0, 0))

    def gather_3(l):
        for dz in (0, 1, 3, 2):
            k = slot(0, 1, dz)
            take(l, k)
            give(l, k, slot(1, 1, dz), device(1, 0, 0))

    def norm(l):
        loads[l].wait()
        wide = 8 * LANES if width % (8 * LANES) == 0 else LANES

        def body(i, acc):
            x = grads[l, :, pl.ds(pl.multiple_of(i * wide, wide), wide)].astype(jnp.float32)
            x = x * x
            for j in range(wide // LANES):
                acc = acc + x[:, LANES * j : LANES * (j + 1)]
            return acc

        acc = lax.fori_loop(0, width // wide, body, jnp.zeros((examples, LANES), jnp.float32))
        each = jnp.sum(acc, axis=1, keepdims=True)
        norms[l] = jnp.broadcast_to(each, (examples, LANES))
        return jnp.broadcast_to(jnp.sum(each, axis=0, keepdims=True), (1, LANES))

    def totals_z():
        for dz in (2, 1, 3):
            at = NZ - dz - 1
            start(total.at[0], totals.at[at], total_send.at[dz - 1], total_recv.at[at], device(0, 0, dz))

    def add_totals(step, first, count):
        acc = total[step]
        for i in range(first, first + count):
            copy(total.at[0], totals.at[i], total_send.at[i], total_recv.at[i], device(0, 1, 0)).wait_recv()
            acc = acc + totals[i]
        return acc

    def totals_y():
        total[1] = add_totals(0, 0, NZ - 1)
        start(total.at[1], totals.at[NZ - 1], total_send.at[NZ - 1], total_recv.at[NZ - 1], device(0, 1, 0))

    def totals_core():
        total[2] = add_totals(1, NZ - 1, 1)
        start(total.at[2], totals.at[NZ], total_send.at[NZ], total_recv.at[NZ], device(1, 0, 0))

    def take_totals():
        return 0.1 * add_totals(2, NZ, 1) / (examples * N)

    def form(l):
        for k in range(N):
            if k:
                take(l, k)
            v_form[pl.ds(k, chunks, stride=N), :] = everything[l, k].astype(jnp.float32)

    def dots(l):
        wide = 2560 if width % 2560 == 0 else width
        acc = jnp.zeros((examples, N), jnp.float32)
        for i in range(width // wide):
            block = jnp.concatenate(
                [v_form[N * j : N * (j + 1), :] for j in range(i * wide // LANES, (i + 1) * wide // LANES)], axis=1
            ).astype(jnp.bfloat16)
            acc = acc + lax.dot_general(
                grads[l, :, i * wide : (i + 1) * wide], block, (((1,), (1,)), ((), ())),
                preferred_element_type=jnp.float32,
            )
        return acc

    def weigh(l, product, damping):
        coef = product / (damping[:, l : l + 1] + norms[l, :, :N])
        coef = coef.T.astype(jnp.bfloat16)
        wide = 1280 if width % 1280 == 0 else width
        for i in range(width // wide):
            result = jnp.dot(coef, grads[l, :, i * wide : (i + 1) * wide], preferred_element_type=jnp.float32)
            for j in range(wide // LANES):
                at = i * wide // LANES + j
                for dc in range(NC):
                    partial[l, dc, HALF * at : HALF * (at + 1), :] = result[HALF * dc : HALF * (dc + 1), LANES * j : LANES * (j + 1)]
        start(partial.at[l, 1], from_core.at[l], core_send.at[l], core_recv.at[l], device(1, 0, 0))

    def scatter_y(l):
        copy(partial.at[l, 1], from_core.at[l], core_send.at[l], core_recv.at[l], device(1, 0, 0)).wait_recv()
        for dz in (2, 1, 3, 0):
            rows = pl.ds(slot(0, 1, dz), chunks, stride=HALF)
            to_y[l, dz] = (partial[l, 0, rows, :] + from_core[l, rows, :]).astype(jnp.bfloat16)
            start(to_y.at[l, dz], from_y.at[l, dz], y_send.at[l, dz], y_recv.at[l, dz], device(0, 1, 0))

    def scatter_z(l):
        for dz in (2, 1, 3, 0):
            copy(
                to_y.at[l, dz], from_y.at[l, dz], y_send.at[l, dz], y_recv.at[l, dz], device(0, 1, 0)
            ).wait_recv()
            rows = pl.ds(slot(0, 0, dz), chunks, stride=HALF)
            part_sum = partial[l, 0, rows, :] + from_core[l, rows, :] + from_y[l, dz].astype(jnp.float32)
            if dz:
                to_z[l, dz - 1] = part_sum.astype(jnp.bfloat16)
                at = NZ - dz - 1
                start(to_z.at[l, dz - 1], from_z.at[l, at], z_send.at[l, dz - 1], z_recv.at[l, at], device(0, 0, dz))
            else:
                mine[l] = part_sum

    def finish(l):
        acc = mine[l]
        for i in range(NZ - 1):
            copy(to_z.at[l, i], from_z.at[l, i], z_send.at[l, i], z_recv.at[l, i], device(0, 1, 0)).wait_recv()
            acc = acc + from_z[l, i].astype(jnp.float32)
        out_ref[l] = acc

    lane = lax.broadcasted_iota(jnp.int32, (1, LANES), 1)
    row = jnp.zeros((1, LANES), jnp.float32)
    for l in range(layers):
        row = jnp.where(lane == l, norm(l), row)
    total[0] = row
    pl.semaphore_wait(barrier, len(offsets))
    gather_1(0)
    totals_z()
    for l in range(1, layers):
        gather_1(l)
    gather_2(0)
    totals_y()
    for l in range(1, layers):
        gather_2(l)
        gather_3(l - 1)
        if l == 1:
            totals_core()
    damping = None
    for l in range(layers):
        form(l)
        product = dots(l)
        if l == 0:
            damping = take_totals()
        else:
            scatter_y(l - 1)
        weigh(l, product, damping)
        if l == 0:
            gather_3(layers - 1)
        if l >= 2:
            scatter_z(l - 2)
    scatter_y(layers - 1)
    for l in range(max(layers - 2, 0), layers):
        scatter_z(l)
    for l in range(layers):
        finish(l)
    for one in sent:
        one.wait_send()


def fused(grads, valid):
    examples, layers, width = grads.shape
    chunks = width // LANES
    bf16, f32 = jnp.bfloat16, jnp.float32
    dma = pltpu.SemaphoreType.DMA
    out = pl.pallas_call(
        kernel,
        out_shape=jax.ShapeDtypeStruct((layers, chunks, LANES), f32),
        in_specs=[pl.BlockSpec(memory_space=pl.ANY), pl.BlockSpec(memory_space=pl.ANY)],
        out_specs=pl.BlockSpec(memory_space=pltpu.VMEM),
        scratch_shapes=[
            pltpu.VMEM((layers, examples, width), bf16),
            pltpu.VMEM((layers, width), bf16),
            pltpu.VMEM((chunks * 8, LANES), f32),
            pltpu.VMEM((layers, N, chunks, LANES), bf16),
            pltpu.VMEM((chunks * N, LANES), f32),
            pltpu.VMEM((layers, examples, LANES), f32),
            pltpu.VMEM((3, 1, LANES), f32),
            pltpu.VMEM((NZ + 1, 1, LANES), f32),
            pltpu.VMEM((layers, NC, chunks * HALF, LANES), f32),
            pltpu.VMEM((layers, chunks * HALF, LANES), f32),
            pltpu.VMEM((layers, NZ, chunks, LANES), bf16),
            pltpu.VMEM((layers, NZ, chunks, LANES), bf16),
            pltpu.VMEM((layers, NZ - 1, chunks, LANES), bf16),
            pltpu.VMEM((layers, NZ - 1, chunks, LANES), bf16),
            pltpu.VMEM((layers, chunks, LANES), f32),
            dma((layers,)),
            dma,
            dma((layers, N)),
            dma((layers, N)),
            dma((NZ + 1,)),
            dma((NZ + 1,)),
            dma((layers,)),
            dma((layers,)),
            dma((layers, NZ)),
            dma((layers, NZ)),
            dma((layers, NZ - 1)),
            dma((layers, NZ - 1)),
        ],
        compiler_params=pltpu.CompilerParams(
            collective_id=0, has_side_effects=True, vmem_limit_bytes=60 * 1024 * 1024
        ),
    )(jnp.transpose(grads, (1, 0, 2)), valid.reshape(layers, width))
    return out.reshape(1, layers, width)


def solution(mesh):
    def step(grads, valid):
        fits = mesh.shape["dp"] == N and valid.shape[0] == 1 and grads.shape[2] % (16 * LANES) == 0
        return (fused if fits else shards)(grads, valid)

    return jax.shard_map(
        step,
        mesh=mesh,
        in_specs=(P(("parts", "dp"), None, None), P(("parts", "dp"), None, None)),
        out_specs=P(("parts", "dp"), None, None),
        check_vma=False,
    )
```

```python
import functools

import jax
import jax.numpy as jnp
from jax import lax
from jax.experimental import pallas as pl
from jax.experimental.pallas import tpu as pltpu
from jax.sharding import PartitionSpec as P

MESH = pl.DeviceIdType.MESH
LANES = 128


def coefficients(grads, block, damping, norms):
    dots = jnp.einsum("elw,vlw->lev", grads, block, preferred_element_type=jnp.float32)
    return (dots / (damping[:, None, None] + norms.T[:, :, None])).astype(jnp.bfloat16)


def shards(grads, valid):
    local_rows = grads.shape[0]
    norms = jnp.einsum("elw,elw->el", grads, grads, preferred_element_type=jnp.float32)
    total = lax.psum(jnp.sum(norms, axis=0), "dp")
    damping = 0.1 * total / (local_rows * lax.axis_size("dp"))
    everything = lax.all_gather(valid, "dp", axis=0, tiled=True)
    coef = coefficients(grads, everything, damping, norms)
    return lax.psum_scatter(
        jnp.einsum("lev,elw->vlw", coef, grads, preferred_element_type=jnp.float32),
        "dp",
        scatter_dimension=0,
        tiled=True,
    )


NC, NY, NZ = 2, 2, 4
N = NC * NY * NZ
HALF = NY * NZ


def slot(dc, dy, dz):
    return (dc * NY + dy) * NZ + dz % NZ


def kernel(
    grads_hbm, valid_hbm, out_ref,
    grads, valid_ref, row_form, everything, v_form, norms, total, totals, partial, from_core, to_y, from_y, to_z, from_z, mine,
    load_sem, valid_sem, gather_send, gather_recv, total_send, total_recv,
    core_send, core_recv, y_send, y_recv, z_send, z_recv,
):
    layers, examples, width = grads_hbm.shape
    chunks = width // LANES
    part, me = lax.axis_index("parts"), lax.axis_index("dp")
    c, y, z = me % NC, (me // NC) % NY, me // (NC * NY)

    def device(dc, dy, dz):
        pc = 1 - c if dc else c
        py = 1 - y if dy else y
        pz = (z + dz) % NZ
        return (part, (pz * NY + py) * NC + pc)

    def copy(src, dst, send, recv, to):
        return pltpu.make_async_remote_copy(
            src_ref=src, dst_ref=dst, send_sem=send, recv_sem=recv, device_id=to, device_id_type=MESH
        )

    sent = []

    def start(*args):
        one = copy(*args)
        one.start()
        sent.append(one)

    offsets = [(0, 0, dz) for dz in (2, 1, 3)] + [(0, 1, 0), (1, 0, 0)]

    barrier = pltpu.get_barrier_semaphore()
    for offset in offsets:
        pl.semaphore_signal(barrier, inc=1, device_id=device(*offset), device_id_type=MESH)

    load_valid = pltpu.make_async_copy(valid_hbm, valid_ref, valid_sem)
    load_valid.start()
    loads = [pltpu.make_async_copy(grads_hbm.at[l], grads.at[l], load_sem.at[l]) for l in range(layers)]
    for load in loads:
        load.start()

    load_valid.wait()
    for j in range(chunks):
        row_form[8 * j : 8 * j + layers, :] = valid_ref[:, LANES * j : LANES * (j + 1)].astype(jnp.float32)
    for l in range(layers):
        everything[l, 0] = row_form[pl.ds(l, chunks, stride=8), :].astype(jnp.bfloat16)

    counter = [0] * layers

    def give(l, src, dst, to):
        start(everything.at[l, src], everything.at[l, dst], gather_send.at[l, counter[l]], gather_recv.at[l, dst], to)
        counter[l] += 1

    arrived = set()

    def take(l, k):
        if (l, k) not in arrived:
            arrived.add((l, k))
            copy(
                everything.at[l, k], everything.at[l, k], gather_send.at[l, 0], gather_recv.at[l, k], device(1, 0, 0)
            ).wait_recv()

    def gather_1(l):
        for dz in (1, 3, 2):
            give(l, 0, slot(0, 0, -dz), device(0, 0, dz))
        give(l, 0, slot(0, 1, 0), device(0, 1, 0))
        give(l, 0, slot(1, 0, 0), device(1, 0, 0))

    def gather_2(l):
        for dz in (1, 3, 2):
            k = slot(0, 0, dz)
            take(l, k)
            give(l, k, slot(0, 1, dz), device(0, 1, 0))
            give(l, k, slot(1, 0, dz), device(1, 0, 0))

    def gather_3(l):
        for dz in (0, 1, 3, 2):
            k = slot(0, 1, dz)
            take(l, k)
            give(l, k, slot(1, 1, dz), device(1, 0, 0))

    def norm(l):
        loads[l].wait()
        wide = 8 * LANES if width % (8 * LANES) == 0 else LANES

        def body(i, acc):
            x = grads[l, :, pl.ds(pl.multiple_of(i * wide, wide), wide)].astype(jnp.float32)
            x = x * x
            for j in range(wide // LANES):
                acc = acc + x[:, LANES * j : LANES * (j + 1)]
            return acc

        acc = lax.fori_loop(0, width // wide, body, jnp.zeros((examples, LANES), jnp.float32))
        each = jnp.sum(acc, axis=1, keepdims=True)
        norms[l] = jnp.broadcast_to(each, (examples, LANES))
        return jnp.broadcast_to(jnp.sum(each, axis=0, keepdims=True), (1, LANES))

    def totals_z():
        for dz in (2, 1, 3):
            at = NZ - dz - 1
            start(total.at[0], totals.at[at], total_send.at[dz - 1], total_recv.at[at], device(0, 0, dz))

    def add_totals(step, first, count):
        acc = total[step]
        for i in range(first, first + count):
            copy(total.at[0], totals.at[i], total_send.at[i], total_recv.at[i], device(0, 1, 0)).wait_recv()
            acc = acc + totals[i]
        return acc

    def totals_y():
        total[1] = add_totals(0, 0, NZ - 1)
        start(total.at[1], totals.at[NZ - 1], total_send.at[NZ - 1], total_recv.at[NZ - 1], device(0, 1, 0))

    def totals_core():
        total[2] = add_totals(1, NZ - 1, 1)
        start(total.at[2], totals.at[NZ], total_send.at[NZ], total_recv.at[NZ], device(1, 0, 0))

    def take_totals():
        return 0.1 * add_totals(2, NZ, 1) / (examples * N)

    def form(l):
        for k in range(N):
            if k:
                take(l, k)
            v_form[pl.ds(k, chunks, stride=N), :] = everything[l, k].astype(jnp.float32)

    def dots(l):
        wide = 2560 if width % 2560 == 0 else width
        acc = jnp.zeros((examples, N), jnp.float32)
        for i in range(width // wide):
            block = jnp.concatenate(
                [v_form[N * j : N * (j + 1), :] for j in range(i * wide // LANES, (i + 1) * wide // LANES)], axis=1
            ).astype(jnp.bfloat16)
            acc = acc + lax.dot_general(
                grads[l, :, i * wide : (i + 1) * wide], block, (((1,), (1,)), ((), ())),
                preferred_element_type=jnp.float32,
            )
        return acc

    def weigh(l, product, damping):
        coef = product / (damping[:, l : l + 1] + norms[l, :, :N])
        coef = coef.T.astype(jnp.bfloat16)
        wide = 1280 if width % 1280 == 0 else width
        for i in range(width // wide):
            result = jnp.dot(coef, grads[l, :, i * wide : (i + 1) * wide], preferred_element_type=jnp.float32)
            for j in range(wide // LANES):
                at = i * wide // LANES + j
                for dc in range(NC):
                    partial[l, dc, HALF * at : HALF * (at + 1), :] = result[HALF * dc : HALF * (dc + 1), LANES * j : LANES * (j + 1)]
        start(partial.at[l, 1], from_core.at[l], core_send.at[l], core_recv.at[l], device(1, 0, 0))

    def scatter_y(l):
        copy(partial.at[l, 1], from_core.at[l], core_send.at[l], core_recv.at[l], device(1, 0, 0)).wait_recv()
        for dz in (3, 1, 2, 0):
            rows = pl.ds(slot(0, 1, dz), chunks, stride=HALF)
            to_y[l, dz] = (partial[l, 0, rows, :] + from_core[l, rows, :]).astype(jnp.bfloat16)
            start(to_y.at[l, dz], from_y.at[l, dz], y_send.at[l, dz], y_recv.at[l, dz], device(0, 1, 0))

    def scatter_z(l):
        for dz in (3, 1, 2, 0):
            copy(
                to_y.at[l, dz], from_y.at[l, dz], y_send.at[l, dz], y_recv.at[l, dz], device(0, 1, 0)
            ).wait_recv()
            rows = pl.ds(slot(0, 0, dz), chunks, stride=HALF)
            part_sum = partial[l, 0, rows, :] + from_core[l, rows, :] + from_y[l, dz].astype(jnp.float32)
            if dz:
                to_z[l, dz - 1] = part_sum.astype(jnp.bfloat16)
                at = NZ - dz - 1
                start(to_z.at[l, dz - 1], from_z.at[l, at], z_send.at[l, dz - 1], z_recv.at[l, at], device(0, 0, dz))
            else:
                mine[l] = part_sum

    def finish(l):
        acc = mine[l]
        for i in range(NZ - 1):
            copy(to_z.at[l, i], from_z.at[l, i], z_send.at[l, i], z_recv.at[l, i], device(0, 1, 0)).wait_recv()
            acc = acc + from_z[l, i].astype(jnp.float32)
        out_ref[l] = acc

    lane = lax.broadcasted_iota(jnp.int32, (1, LANES), 1)
    row = jnp.zeros((1, LANES), jnp.float32)
    for l in range(layers - 1):
        row = jnp.where(lane == l, norm(l), row)
    pl.semaphore_wait(barrier, len(offsets))
    gather_1(0)
    total[0] = jnp.where(lane == layers - 1, norm(layers - 1), row)
    totals_z()
    for l in range(1, layers):
        gather_1(l)
    gather_2(0)
    totals_y()
    for l in range(1, layers):
        gather_2(l)
        gather_3(l - 1)
        if l == 1:
            totals_core()
    damping = None
    for l in range(layers):
        form(l)
        product = dots(l)
        if l == 0:
            damping = take_totals()
        else:
            scatter_y(l - 1)
        weigh(l, product, damping)
        if l == 0:
            gather_3(layers - 1)
        if l >= 2:
            scatter_z(l - 2)
    scatter_y(layers - 1)
    for l in range(max(layers - 2, 0), layers):
        scatter_z(l)
    for l in range(layers):
        finish(l)
    for one in sent:
        one.wait_send()


def fused(grads, valid):
    examples, layers, width = grads.shape
    chunks = width // LANES
    bf16, f32 = jnp.bfloat16, jnp.float32
    dma = pltpu.SemaphoreType.DMA
    out = pl.pallas_call(
        kernel,
        out_shape=jax.ShapeDtypeStruct((layers, chunks, LANES), f32),
        in_specs=[pl.BlockSpec(memory_space=pl.ANY), pl.BlockSpec(memory_space=pl.ANY)],
        out_specs=pl.BlockSpec(memory_space=pltpu.VMEM),
        scratch_shapes=[
            pltpu.VMEM((layers, examples, width), bf16),
            pltpu.VMEM((layers, width), bf16),
            pltpu.VMEM((chunks * 8, LANES), f32),
            pltpu.VMEM((layers, N, chunks, LANES), bf16),
            pltpu.VMEM((chunks * N, LANES), f32),
            pltpu.VMEM((layers, examples, LANES), f32),
            pltpu.VMEM((3, 1, LANES), f32),
            pltpu.VMEM((NZ + 1, 1, LANES), f32),
            pltpu.VMEM((layers, NC, chunks * HALF, LANES), f32),
            pltpu.VMEM((layers, chunks * HALF, LANES), f32),
            pltpu.VMEM((layers, NZ, chunks, LANES), bf16),
            pltpu.VMEM((layers, NZ, chunks, LANES), bf16),
            pltpu.VMEM((layers, NZ - 1, chunks, LANES), bf16),
            pltpu.VMEM((layers, NZ - 1, chunks, LANES), bf16),
            pltpu.VMEM((layers, chunks, LANES), f32),
            dma((layers,)),
            dma,
            dma((layers, N)),
            dma((layers, N)),
            dma((NZ + 1,)),
            dma((NZ + 1,)),
            dma((layers,)),
            dma((layers,)),
            dma((layers, NZ)),
            dma((layers, NZ)),
            dma((layers, NZ - 1)),
            dma((layers, NZ - 1)),
        ],
        compiler_params=pltpu.CompilerParams(
            collective_id=0, has_side_effects=True, vmem_limit_bytes=60 * 1024 * 1024
        ),
    )(jnp.transpose(grads, (1, 0, 2)), valid.reshape(layers, width))
    return out.reshape(1, layers, width)


def solution(mesh):
    def step(grads, valid):
        fits = mesh.shape["dp"] == N and valid.shape[0] == 1 and grads.shape[2] % (16 * LANES) == 0
        return (fused if fits else shards)(grads, valid)

    return jax.shard_map(
        step,
        mesh=mesh,
        in_specs=(P(("parts", "dp"), None, None), P(("parts", "dp"), None, None)),
        out_specs=P(("parts", "dp"), None, None),
        check_vma=False,
    )
```

```python
import functools

import jax
import jax.numpy as jnp
from jax import lax
from jax.experimental import pallas as pl
from jax.experimental.pallas import tpu as pltpu
from jax.sharding import PartitionSpec as P

MESH = pl.DeviceIdType.MESH
LANES = 128


def coefficients(grads, block, damping, norms):
    dots = jnp.einsum("elw,vlw->lev", grads, block, preferred_element_type=jnp.float32)
    return (dots / (damping[:, None, None] + norms.T[:, :, None])).astype(jnp.bfloat16)


def shards(grads, valid):
    local_rows = grads.shape[0]
    norms = jnp.einsum("elw,elw->el", grads, grads, preferred_element_type=jnp.float32)
    total = lax.psum(jnp.sum(norms, axis=0), "dp")
    damping = 0.1 * total / (local_rows * lax.axis_size("dp"))
    everything = lax.all_gather(valid, "dp", axis=0, tiled=True)
    coef = coefficients(grads, everything, damping, norms)
    return lax.psum_scatter(
        jnp.einsum("lev,elw->vlw", coef, grads, preferred_element_type=jnp.float32),
        "dp",
        scatter_dimension=0,
        tiled=True,
    )


NC, NY, NZ = 2, 2, 4
N = NC * NY * NZ
HALF = NY * NZ


def slot(dc, dy, dz):
    return (dc * NY + dy) * NZ + dz % NZ


def kernel(
    grads_hbm, valid_hbm, out_ref,
    grads, valid_ref, row_form, everything, v_form, norms, total, totals, partial, from_core, to_y, from_y, to_z, from_z, mine,
    load_sem, valid_sem, gather_send, gather_recv, total_send, total_recv,
    core_send, core_recv, y_send, y_recv, z_send, z_recv,
):
    layers, examples, width = grads_hbm.shape
    chunks = width // LANES
    part, me = lax.axis_index("parts"), lax.axis_index("dp")
    c, y, z = me % NC, (me // NC) % NY, me // (NC * NY)

    def device(dc, dy, dz):
        pc = 1 - c if dc else c
        py = 1 - y if dy else y
        pz = (z + dz) % NZ
        return (part, (pz * NY + py) * NC + pc)

    def copy(src, dst, send, recv, to):
        return pltpu.make_async_remote_copy(
            src_ref=src, dst_ref=dst, send_sem=send, recv_sem=recv, device_id=to, device_id_type=MESH
        )

    sent = []

    def start(*args):
        one = copy(*args)
        one.start()
        sent.append(one)

    offsets = [(0, 0, dz) for dz in (2, 1, 3)] + [(0, 1, 0), (1, 0, 0)]

    barrier = pltpu.get_barrier_semaphore()
    for offset in offsets:
        pl.semaphore_signal(barrier, inc=1, device_id=device(*offset), device_id_type=MESH)

    load_valid = pltpu.make_async_copy(valid_hbm, valid_ref, valid_sem)
    load_valid.start()
    loads = [pltpu.make_async_copy(grads_hbm.at[l], grads.at[l], load_sem.at[l]) for l in range(layers)]
    for load in loads:
        load.start()

    load_valid.wait()
    for j in range(chunks):
        row_form[8 * j : 8 * j + layers, :] = valid_ref[:, LANES * j : LANES * (j + 1)].astype(jnp.float32)
    for l in range(layers):
        everything[l, 0] = row_form[pl.ds(l, chunks, stride=8), :].astype(jnp.bfloat16)

    counter = [0] * layers

    def give(l, src, dst, to):
        start(everything.at[l, src], everything.at[l, dst], gather_send.at[l, counter[l]], gather_recv.at[l, dst], to)
        counter[l] += 1

    arrived = set()

    def take(l, k):
        if (l, k) not in arrived:
            arrived.add((l, k))
            copy(
                everything.at[l, k], everything.at[l, k], gather_send.at[l, 0], gather_recv.at[l, k], device(1, 0, 0)
            ).wait_recv()

    def gather_1(l):
        for dz in (1, 3, 2):
            give(l, 0, slot(0, 0, -dz), device(0, 0, dz))
        give(l, 0, slot(0, 1, 0), device(0, 1, 0))
        give(l, 0, slot(1, 0, 0), device(1, 0, 0))

    def gather_2(l):
        for dz in (1, 3, 2):
            k = slot(0, 0, dz)
            take(l, k)
            give(l, k, slot(0, 1, dz), device(0, 1, 0))
            give(l, k, slot(1, 0, dz), device(1, 0, 0))

    def gather_3(l):
        for dz in (0, 1, 3, 2):
            k = slot(0, 1, dz)
            take(l, k)
            give(l, k, slot(1, 1, dz), device(1, 0, 0))

    def norm(l):
        loads[l].wait()
        wide = 8 * LANES if width % (8 * LANES) == 0 else LANES

        def body(i, acc):
            x = grads[l, :, pl.ds(pl.multiple_of(i * wide, wide), wide)].astype(jnp.float32)
            x = x * x
            for j in range(wide // LANES):
                acc = acc + x[:, LANES * j : LANES * (j + 1)]
            return acc

        acc = lax.fori_loop(0, width // wide, body, jnp.zeros((examples, LANES), jnp.float32))
        each = jnp.sum(acc, axis=1, keepdims=True)
        norms[l] = jnp.broadcast_to(each, (examples, LANES))
        return jnp.broadcast_to(jnp.sum(each, axis=0, keepdims=True), (1, LANES))

    def totals_z():
        for dz in (2, 1, 3):
            at = NZ - dz - 1
            start(total.at[0], totals.at[at], total_send.at[dz - 1], total_recv.at[at], device(0, 0, dz))

    def add_totals(step, first, count):
        acc = total[step]
        for i in range(first, first + count):
            copy(total.at[0], totals.at[i], total_send.at[i], total_recv.at[i], device(0, 1, 0)).wait_recv()
            acc = acc + totals[i]
        return acc

    def totals_y():
        total[1] = add_totals(0, 0, NZ - 1)
        start(total.at[1], totals.at[NZ - 1], total_send.at[NZ - 1], total_recv.at[NZ - 1], device(0, 1, 0))

    def totals_core():
        total[2] = add_totals(1, NZ - 1, 1)
        start(total.at[2], totals.at[NZ], total_send.at[NZ], total_recv.at[NZ], device(1, 0, 0))

    def take_totals():
        return 0.1 * add_totals(2, NZ, 1) / (examples * N)

    def form(l):
        for k in range(N):
            if k:
                take(l, k)
            v_form[pl.ds(k, chunks, stride=N), :] = everything[l, k].astype(jnp.float32)

    def dots(l):
        wide = 2560 if width % 2560 == 0 else width
        acc = jnp.zeros((examples, N), jnp.float32)
        for i in range(width // wide):
            block = jnp.concatenate(
                [v_form[N * j : N * (j + 1), :] for j in range(i * wide // LANES, (i + 1) * wide // LANES)], axis=1
            ).astype(jnp.bfloat16)
            acc = acc + lax.dot_general(
                grads[l, :, i * wide : (i + 1) * wide], block, (((1,), (1,)), ((), ())),
                preferred_element_type=jnp.float32,
            )
        return acc

    def weigh(l, product, damping):
        coef = product / (damping[:, l : l + 1] + norms[l, :, :N])
        coef = coef.T.astype(jnp.bfloat16)
        wide = 1280 if width % 1280 == 0 else width
        for i in range(width // wide):
            result = jnp.dot(coef, grads[l, :, i * wide : (i + 1) * wide], preferred_element_type=jnp.float32)
            for j in range(wide // LANES):
                at = i * wide // LANES + j
                for dc in range(NC):
                    partial[l, dc, HALF * at : HALF * (at + 1), :] = result[HALF * dc : HALF * (dc + 1), LANES * j : LANES * (j + 1)]
        start(partial.at[l, 1], from_core.at[l], core_send.at[l], core_recv.at[l], device(1, 0, 0))

    def scatter_y(l):
        copy(partial.at[l, 1], from_core.at[l], core_send.at[l], core_recv.at[l], device(1, 0, 0)).wait_recv()
        for dz in (3, 1, 2, 0):
            rows = pl.ds(slot(0, 1, dz), chunks, stride=HALF)
            to_y[l, dz] = (partial[l, 0, rows, :] + from_core[l, rows, :]).astype(jnp.bfloat16)
            start(to_y.at[l, dz], from_y.at[l, dz], y_send.at[l, dz], y_recv.at[l, dz], device(0, 1, 0))

    def scatter_z(l):
        for dz in (3, 1, 2, 0):
            copy(
                to_y.at[l, dz], from_y.at[l, dz], y_send.at[l, dz], y_recv.at[l, dz], device(0, 1, 0)
            ).wait_recv()
            rows = pl.ds(slot(0, 0, dz), chunks, stride=HALF)
            part_sum = partial[l, 0, rows, :] + from_core[l, rows, :] + from_y[l, dz].astype(jnp.float32)
            if dz:
                to_z[l, dz - 1] = part_sum.astype(jnp.bfloat16)
                at = NZ - dz - 1
                start(to_z.at[l, dz - 1], from_z.at[l, at], z_send.at[l, dz - 1], z_recv.at[l, at], device(0, 0, dz))
            else:
                mine[l] = part_sum

    def finish(l):
        acc = mine[l]
        for i in range(NZ - 1):
            copy(to_z.at[l, i], from_z.at[l, i], z_send.at[l, i], z_recv.at[l, i], device(0, 1, 0)).wait_recv()
            acc = acc + from_z[l, i].astype(jnp.float32)
        out_ref[l] = acc

    lane = lax.broadcasted_iota(jnp.int32, (1, LANES), 1)
    row = jnp.zeros((1, LANES), jnp.float32)
    for l in range(layers - 1):
        row = jnp.where(lane == l, norm(l), row)
    pl.semaphore_wait(barrier, len(offsets))
    gather_1(0)
    total[0] = jnp.where(lane == layers - 1, norm(layers - 1), row)
    totals_z()
    for l in range(1, layers):
        gather_1(l)
    gather_2(0)
    totals_y()
    for l in range(1, layers):
        gather_2(l)
        gather_3(l - 1)
        if l == 1:
            totals_core()
    damping = None
    for l in range(layers):
        form(l)
        product = dots(l)
        if l == 0:
            damping = take_totals()
        weigh(l, product, damping)
        if l:
            scatter_y(l - 1)
        if l == 0:
            gather_3(layers - 1)
        if l >= 2:
            scatter_z(l - 2)
    scatter_y(layers - 1)
    for l in range(max(layers - 2, 0), layers):
        scatter_z(l)
    for l in range(layers):
        finish(l)
    for one in sent:
        one.wait_send()


def fused(grads, valid):
    examples, layers, width = grads.shape
    chunks = width // LANES
    bf16, f32 = jnp.bfloat16, jnp.float32
    dma = pltpu.SemaphoreType.DMA
    out = pl.pallas_call(
        kernel,
        out_shape=jax.ShapeDtypeStruct((layers, chunks, LANES), f32),
        in_specs=[pl.BlockSpec(memory_space=pl.ANY), pl.BlockSpec(memory_space=pl.ANY)],
        out_specs=pl.BlockSpec(memory_space=pltpu.VMEM),
        scratch_shapes=[
            pltpu.VMEM((layers, examples, width), bf16),
            pltpu.VMEM((layers, width), bf16),
            pltpu.VMEM((chunks * 8, LANES), f32),
            pltpu.VMEM((layers, N, chunks, LANES), bf16),
            pltpu.VMEM((chunks * N, LANES), f32),
            pltpu.VMEM((layers, examples, LANES), f32),
            pltpu.VMEM((3, 1, LANES), f32),
            pltpu.VMEM((NZ + 1, 1, LANES), f32),
            pltpu.VMEM((layers, NC, chunks * HALF, LANES), f32),
            pltpu.VMEM((layers, chunks * HALF, LANES), f32),
            pltpu.VMEM((layers, NZ, chunks, LANES), bf16),
            pltpu.VMEM((layers, NZ, chunks, LANES), bf16),
            pltpu.VMEM((layers, NZ - 1, chunks, LANES), bf16),
            pltpu.VMEM((layers, NZ - 1, chunks, LANES), bf16),
            pltpu.VMEM((layers, chunks, LANES), f32),
            dma((layers,)),
            dma,
            dma((layers, N)),
            dma((layers, N)),
            dma((NZ + 1,)),
            dma((NZ + 1,)),
            dma((layers,)),
            dma((layers,)),
            dma((layers, NZ)),
            dma((layers, NZ)),
            dma((layers, NZ - 1)),
            dma((layers, NZ - 1)),
        ],
        compiler_params=pltpu.CompilerParams(
            collective_id=0, has_side_effects=True, vmem_limit_bytes=60 * 1024 * 1024
        ),
    )(jnp.transpose(grads, (1, 0, 2)), valid.reshape(layers, width))
    return out.reshape(1, layers, width)


def solution(mesh):
    def step(grads, valid):
        fits = mesh.shape["dp"] == N and valid.shape[0] == 1 and grads.shape[2] % (16 * LANES) == 0
        return (fused if fits else shards)(grads, valid)

    return jax.shard_map(
        step,
        mesh=mesh,
        in_specs=(P(("parts", "dp"), None, None), P(("parts", "dp"), None, None)),
        out_specs=P(("parts", "dp"), None, None),
        check_vma=False,
    )
```

```python
import functools

import jax
import jax.numpy as jnp
from jax import lax
from jax.experimental import pallas as pl
from jax.experimental.pallas import tpu as pltpu
from jax.sharding import PartitionSpec as P

MESH = pl.DeviceIdType.MESH
LANES = 128


def coefficients(grads, block, damping, norms):
    dots = jnp.einsum("elw,vlw->lev", grads, block, preferred_element_type=jnp.float32)
    return (dots / (damping[:, None, None] + norms.T[:, :, None])).astype(jnp.bfloat16)


def shards(grads, valid):
    local_rows = grads.shape[0]
    norms = jnp.einsum("elw,elw->el", grads, grads, preferred_element_type=jnp.float32)
    total = lax.psum(jnp.sum(norms, axis=0), "dp")
    damping = 0.1 * total / (local_rows * lax.axis_size("dp"))
    everything = lax.all_gather(valid, "dp", axis=0, tiled=True)
    coef = coefficients(grads, everything, damping, norms)
    return lax.psum_scatter(
        jnp.einsum("lev,elw->vlw", coef, grads, preferred_element_type=jnp.float32),
        "dp",
        scatter_dimension=0,
        tiled=True,
    )


NC, NY, NZ = 2, 2, 4
N = NC * NY * NZ
HALF = NY * NZ


def slot(dc, dy, dz):
    return (dc * NY + dy) * NZ + dz % NZ


def kernel(
    grads_hbm, valid_hbm, out_ref,
    grads, valid_ref, row_form, everything, v_form, norms, total, totals, partial, from_core, to_y, from_y, to_z, from_z, mine,
    load_sem, valid_sem, gather_send, gather_recv, total_send, total_recv,
    core_send, core_recv, y_send, y_recv, z_send, z_recv,
):
    layers, examples, width = grads_hbm.shape
    chunks = width // LANES
    part, me = lax.axis_index("parts"), lax.axis_index("dp")
    c, y, z = me % NC, (me // NC) % NY, me // (NC * NY)

    def device(dc, dy, dz):
        pc = 1 - c if dc else c
        py = 1 - y if dy else y
        pz = (z + dz) % NZ
        return (part, (pz * NY + py) * NC + pc)

    def copy(src, dst, send, recv, to):
        return pltpu.make_async_remote_copy(
            src_ref=src, dst_ref=dst, send_sem=send, recv_sem=recv, device_id=to, device_id_type=MESH
        )

    sent = []

    def start(*args):
        one = copy(*args)
        one.start()
        sent.append(one)

    offsets = [(0, 0, dz) for dz in (2, 1, 3)] + [(0, 1, 0), (1, 0, 0)]

    barrier = pltpu.get_barrier_semaphore()
    for offset in offsets:
        pl.semaphore_signal(barrier, inc=1, device_id=device(*offset), device_id_type=MESH)

    load_valid = pltpu.make_async_copy(valid_hbm, valid_ref, valid_sem)
    load_valid.start()
    loads = [pltpu.make_async_copy(grads_hbm.at[l], grads.at[l], load_sem.at[l]) for l in range(layers)]
    for load in loads:
        load.start()

    load_valid.wait()
    for j in range(chunks):
        row_form[8 * j : 8 * j + layers, :] = valid_ref[:, LANES * j : LANES * (j + 1)].astype(jnp.float32)
    for l in range(layers):
        everything[l, 0] = row_form[pl.ds(l, chunks, stride=8), :].astype(jnp.bfloat16)

    counter = [0] * layers

    def give(l, src, dst, to):
        start(everything.at[l, src], everything.at[l, dst], gather_send.at[l, counter[l]], gather_recv.at[l, dst], to)
        counter[l] += 1

    arrived = set()

    def take(l, k):
        if (l, k) not in arrived:
            arrived.add((l, k))
            copy(
                everything.at[l, k], everything.at[l, k], gather_send.at[l, 0], gather_recv.at[l, k], device(1, 0, 0)
            ).wait_recv()

    def gather_1(l):
        for dz in (1, 3, 2):
            give(l, 0, slot(0, 0, -dz), device(0, 0, dz))

    def gather_1_near(l):
        give(l, 0, slot(0, 1, 0), device(0, 1, 0))
        give(l, 0, slot(1, 0, 0), device(1, 0, 0))

    def gather_2(l):
        for dz in (1, 3, 2):
            k = slot(0, 0, dz)
            take(l, k)
            give(l, k, slot(0, 1, dz), device(0, 1, 0))
            give(l, k, slot(1, 0, dz), device(1, 0, 0))

    def gather_3(l):
        for dz in (0, 1, 3, 2):
            k = slot(0, 1, dz)
            take(l, k)
            give(l, k, slot(1, 1, dz), device(1, 0, 0))

    def norm(l):
        loads[l].wait()
        wide = 8 * LANES if width % (8 * LANES) == 0 else LANES

        def body(i, acc):
            x = grads[l, :, pl.ds(pl.multiple_of(i * wide, wide), wide)].astype(jnp.float32)
            x = x * x
            for j in range(wide // LANES):
                acc = acc + x[:, LANES * j : LANES * (j + 1)]
            return acc

        acc = lax.fori_loop(0, width // wide, body, jnp.zeros((examples, LANES), jnp.float32))
        each = jnp.sum(acc, axis=1, keepdims=True)
        norms[l] = jnp.broadcast_to(each, (examples, LANES))
        return jnp.broadcast_to(jnp.sum(each, axis=0, keepdims=True), (1, LANES))

    def totals_z():
        for dz in (2, 1, 3):
            at = NZ - dz - 1
            start(total.at[0], totals.at[at], total_send.at[dz - 1], total_recv.at[at], device(0, 0, dz))

    def add_totals(step, first, count):
        acc = total[step]
        for i in range(first, first + count):
            copy(total.at[0], totals.at[i], total_send.at[i], total_recv.at[i], device(0, 1, 0)).wait_recv()
            acc = acc + totals[i]
        return acc

    def totals_y():
        total[1] = add_totals(0, 0, NZ - 1)
        start(total.at[1], totals.at[NZ - 1], total_send.at[NZ - 1], total_recv.at[NZ - 1], device(0, 1, 0))

    def totals_core():
        total[2] = add_totals(1, NZ - 1, 1)
        start(total.at[2], totals.at[NZ], total_send.at[NZ], total_recv.at[NZ], device(1, 0, 0))

    def take_totals():
        return 0.1 * add_totals(2, NZ, 1) / (examples * N)

    def form(l):
        for k in range(N):
            if k:
                take(l, k)
            v_form[pl.ds(k, chunks, stride=N), :] = everything[l, k].astype(jnp.float32)

    def dots(l):
        wide = 2560 if width % 2560 == 0 else width
        acc = jnp.zeros((examples, N), jnp.float32)
        for i in range(width // wide):
            block = jnp.concatenate(
                [v_form[N * j : N * (j + 1), :] for j in range(i * wide // LANES, (i + 1) * wide // LANES)], axis=1
            ).astype(jnp.bfloat16)
            acc = acc + lax.dot_general(
                grads[l, :, i * wide : (i + 1) * wide], block, (((1,), (1,)), ((), ())),
                preferred_element_type=jnp.float32,
            )
        return acc

    def weigh(l, product, damping):
        coef = product / (damping[:, l : l + 1] + norms[l, :, :N])
        coef = coef.T.astype(jnp.bfloat16)
        wide = 1280 if width % 1280 == 0 else width
        for i in range(width // wide):
            result = jnp.dot(coef, grads[l, :, i * wide : (i + 1) * wide], preferred_element_type=jnp.float32)
            for j in range(wide // LANES):
                at = i * wide // LANES + j
                for dc in range(NC):
                    partial[l, dc, HALF * at : HALF * (at + 1), :] = result[HALF * dc : HALF * (dc + 1), LANES * j : LANES * (j + 1)]
        start(partial.at[l, 1], from_core.at[l], core_send.at[l], core_recv.at[l], device(1, 0, 0))

    def scatter_y(l):
        copy(partial.at[l, 1], from_core.at[l], core_send.at[l], core_recv.at[l], device(1, 0, 0)).wait_recv()
        for dz in (3, 1, 2, 0):
            rows = pl.ds(slot(0, 1, dz), chunks, stride=HALF)
            to_y[l, dz] = (partial[l, 0, rows, :] + from_core[l, rows, :]).astype(jnp.bfloat16)
            start(to_y.at[l, dz], from_y.at[l, dz], y_send.at[l, dz], y_recv.at[l, dz], device(0, 1, 0))

    def scatter_z(l):
        for dz in (3, 1, 2, 0):
            copy(
                to_y.at[l, dz], from_y.at[l, dz], y_send.at[l, dz], y_recv.at[l, dz], device(0, 1, 0)
            ).wait_recv()
            rows = pl.ds(slot(0, 0, dz), chunks, stride=HALF)
            part_sum = partial[l, 0, rows, :] + from_core[l, rows, :] + from_y[l, dz].astype(jnp.float32)
            if dz:
                to_z[l, dz - 1] = part_sum.astype(jnp.bfloat16)
                at = NZ - dz - 1
                start(to_z.at[l, dz - 1], from_z.at[l, at], z_send.at[l, dz - 1], z_recv.at[l, at], device(0, 0, dz))
            else:
                mine[l] = part_sum

    def finish(l):
        acc = mine[l]
        for i in range(NZ - 1):
            copy(to_z.at[l, i], from_z.at[l, i], z_send.at[l, i], z_recv.at[l, i], device(0, 1, 0)).wait_recv()
            acc = acc + from_z[l, i].astype(jnp.float32)
        out_ref[l] = acc

    lane = lax.broadcasted_iota(jnp.int32, (1, LANES), 1)
    row = jnp.zeros((1, LANES), jnp.float32)
    for l in range(layers - 1):
        row = jnp.where(lane == l, norm(l), row)
    pl.semaphore_wait(barrier, len(offsets))
    gather_1(0)
    for l in range(layers):
        gather_1_near(l)
    total[0] = jnp.where(lane == layers - 1, norm(layers - 1), row)
    totals_z()
    for l in range(1, layers):
        gather_1(l)
    gather_2(0)
    totals_y()
    for l in range(1, layers):
        gather_2(l)
        gather_3(l - 1)
        if l == 1:
            totals_core()
    damping = None
    for l in range(layers):
        form(l)
        product = dots(l)
        if l == 0:
            damping = take_totals()
        weigh(l, product, damping)
        if l:
            scatter_y(l - 1)
        if l == 0:
            gather_3(layers - 1)
        if l >= 2:
            scatter_z(l - 2)
    scatter_y(layers - 1)
    for l in range(max(layers - 2, 0), layers):
        scatter_z(l)
    for l in range(layers):
        finish(l)
    for one in sent:
        one.wait_send()


def fused(grads, valid):
    examples, layers, width = grads.shape
    chunks = width // LANES
    bf16, f32 = jnp.bfloat16, jnp.float32
    dma = pltpu.SemaphoreType.DMA
    out = pl.pallas_call(
        kernel,
        out_shape=jax.ShapeDtypeStruct((layers, chunks, LANES), f32),
        in_specs=[pl.BlockSpec(memory_space=pl.ANY), pl.BlockSpec(memory_space=pl.ANY)],
        out_specs=pl.BlockSpec(memory_space=pltpu.VMEM),
        scratch_shapes=[
            pltpu.VMEM((layers, examples, width), bf16),
            pltpu.VMEM((layers, width), bf16),
            pltpu.VMEM((chunks * 8, LANES), f32),
            pltpu.VMEM((layers, N, chunks, LANES), bf16),
            pltpu.VMEM((chunks * N, LANES), f32),
            pltpu.VMEM((layers, examples, LANES), f32),
            pltpu.VMEM((3, 1, LANES), f32),
            pltpu.VMEM((NZ + 1, 1, LANES), f32),
            pltpu.VMEM((layers, NC, chunks * HALF, LANES), f32),
            pltpu.VMEM((layers, chunks * HALF, LANES), f32),
            pltpu.VMEM((layers, NZ, chunks, LANES), bf16),
            pltpu.VMEM((layers, NZ, chunks, LANES), bf16),
            pltpu.VMEM((layers, NZ - 1, chunks, LANES), bf16),
            pltpu.VMEM((layers, NZ - 1, chunks, LANES), bf16),
            pltpu.VMEM((layers, chunks, LANES), f32),
            dma((layers,)),
            dma,
            dma((layers, N)),
            dma((layers, N)),
            dma((NZ + 1,)),
            dma((NZ + 1,)),
            dma((layers,)),
            dma((layers,)),
            dma((layers, NZ)),
            dma((layers, NZ)),
            dma((layers, NZ - 1)),
            dma((layers, NZ - 1)),
        ],
        compiler_params=pltpu.CompilerParams(
            collective_id=0, has_side_effects=True, vmem_limit_bytes=60 * 1024 * 1024
        ),
    )(jnp.transpose(grads, (1, 0, 2)), valid.reshape(layers, width))
    return out.reshape(1, layers, width)


def solution(mesh):
    def step(grads, valid):
        fits = mesh.shape["dp"] == N and valid.shape[0] == 1 and grads.shape[2] % (16 * LANES) == 0
        return (fused if fits else shards)(grads, valid)

    return jax.shard_map(
        step,
        mesh=mesh,
        in_specs=(P(("parts", "dp"), None, None), P(("parts", "dp"), None, None)),
        out_specs=P(("parts", "dp"), None, None),
        check_vma=False,
    )
```
